512 devices in a mesh: row: 16 (over y, x), col: 32 (over z, core).
Axes of the slice: x: 4, y: 4, z: 16, core: 2. Of those that a mesh axis runs over, the one named last changes fastest.
Arguments:
- tensor: float32 [32, 4096, 4096], P(None, 'row', 'col'), may hold values from -82 to 82
- old_factor: float32 [4096, 32], P('row'), may hold values from -0.09375 to 0.09375
- factor_two: float32 [4096, 32], P('col'), may hold values from -0.09375 to 0.09375
- factor_three: float32 [32, 32], replicated, may hold values from -1 to 1
Outputs:
- new_factor: float32 [4096, 32], P('row')
- core: float32 [32, 1024], P(None, 'col')
The draws below stay inside these ranges and needn't reach their ends.
All inputs are finite; a program needn't handle non-finite values.
Results may differ from the reference program's by a relative error of at most 0.0003.
Values sent between devices are 32-bit elements; how exact they have to be, the bound alone decides.
No kernel may reach another device: no remote copies, remote signals or barrier semaphores. Data moves between devices by JAX's collectives and lax.ppermute only.
A program may use at most 64 MiB of HBM per device.

```python
import math
import jax
import jax.numpy as jnp
from jax import lax

I1 = 4096
I2 = 4096
I3 = 32
RANK = 32
ITERS = 2


def draw_tensor(key, part):
    first, second = jax.random.split(key, 2)
    position = jnp.arange(I1, dtype=jnp.float32) / I1
    rising = jnp.exp(jnp.log(3.0) * position)
    spread = jnp.exp(jax.random.uniform(second, (I1,), dtype=jnp.float32, minval=0.0, maxval=jnp.log(4.0)))
    scales = rising * spread
    base = jnp.clip(jax.random.normal(first, (I3, I1, I2), dtype=jnp.float32), -6.0, 6.0)
    return base * scales[None, :, None]


def levels(rng, shape, pieces, smallest, largest):
    loudness = 1.0
    for dim, blocks in pieces:
        heights = jax.random.uniform(jax.random.fold_in(jax.random.fold_in(rng, 6), dim), (blocks,), jnp.float32, smallest / len(pieces), largest / len(pieces))
        loudness = loudness * jnp.repeat(jnp.exp(heights), shape[dim] // blocks).reshape((-1,) + (1,) * (len(shape) - 1 - dim))
    return loudness


def noise(stream_key, shape, width, reach, shards=(), kind=jnp.bfloat16):
    result = jax.random.normal(stream_key, shape, jnp.float32) * width
    if len(shards) > 0:
        result = levels(stream_key, shape, shards, -0.22, 0.18) * result
    return jnp.clip(result, min=-reach, max=reach).astype(kind)


def setup_inputs(seed: int = 0) -> dict:
    streams_of = jax.random.split(jax.random.key(seed), 5)
    return {
        "tensor": draw_tensor(jax.random.fold_in(streams_of[4], 71), 0),
        "old_factor": noise(streams_of[1], (I1, RANK), I1 ** -0.5, 0.09375, ((0, 16),), jnp.float32),
        "factor_two": noise(streams_of[2], (I2, RANK), I2 ** -0.5, 0.09375, ((0, 32),), jnp.float32),
        "factor_three": noise(streams_of[3], (I3, RANK), I3 ** -0.5, 1.0, (), jnp.float32),
    }


def right_solve(lower, matrix):
    return lax.linalg.triangular_solve(lower, matrix, left_side=False, lower=True, transpose_a=True)

def orthonormal(gram, image):
    lower = jnp.linalg.cholesky(gram)
    return right_solve(lower, image)

def reference(tensor, old_factor, factor_two, factor_three):
    highest = lax.Precision.HIGHEST
    block = min(I1, 256)
    count = I1 // block

    def one_block(index):
        start = (index * block).astype(jnp.int32)
        piece = lax.dynamic_slice_in_dim(tensor, start, block, 1)
        third = jnp.einsum('kij,kb->bij', piece, factor_three, precision=highest)
        return jnp.einsum('bij,ja->iab', third, factor_two, precision=highest).reshape(block, RANK * RANK)
    unfolded = lax.map(one_block, jnp.arange(count, dtype=jnp.int32)).reshape(I1, RANK * RANK)
    factor = old_factor
    coeffs = jnp.dot(unfolded.T, factor, precision=highest)
    for step in range(ITERS):
        image = jnp.dot(unfolded, coeffs, precision=highest)
        gram = jnp.dot(image.T, image, precision=highest)
        factor = orthonormal(gram, image)
        coeffs = jnp.dot(unfolded.T, factor, precision=highest)
    return (factor * math.sqrt(I1), coeffs.T)
```

```python
import functools
import math

import jax
import jax.numpy as jnp
from jax import lax
from jax.experimental import pallas as pl
from jax.experimental.pallas import tpu as pltpu
from jax.sharding import PartitionSpec as P

I1 = 4096
RANK = 32
NEAR = 4
FAR = 4
ROWS = 256
COLS = 128
HIGHEST = lax.Precision.HIGHEST
F32 = jnp.float32
BF16 = jnp.bfloat16


def nn(a, b):
    return lax.dot_general(a, b, (((1,), (0,)), ((), ())), precision=HIGHEST, preferred_element_type=F32)


def nt(a, b):
    return lax.dot_general(a, b, (((1,), (1,)), ((), ())), precision=HIGHEST, preferred_element_type=F32)


def pack(square):
    return jnp.concatenate([square[8 * q : 8 * q + 8] for q in range(4)], axis=1)


def unpack(packed):
    return jnp.concatenate([packed[:, 32 * q : 32 * q + 32] for q in range(4)], axis=0)


def widen(packed):
    return jnp.concatenate([packed, jnp.zeros_like(packed)], axis=1)


def lower_solve(gram, sides):
    row_of = lax.broadcasted_iota(jnp.int32, (RANK, 1), 0)
    diagonal = jnp.zeros((RANK, 1), F32)
    for j in range(RANK):
        column = gram[:, j : j + 1]
        pivot = column[j : j + 1, :]
        diagonal = jnp.where(row_of == j, pivot, diagonal)
        factor = jnp.where(row_of > j, column, 0.0) / pivot
        sides = [side - factor * side[j : j + 1, :] for side in sides]
        gram = gram - factor * gram[j : j + 1, :]
    scale = lax.rsqrt(diagonal)
    return [side * scale for side in sides]


def contract_kernel(core_ref, factor_ref, tensor_ref, keep_ref, send_ref, left_ref, right_ref):
    depth = tensor_ref.shape[0]
    core = core_ref[0]
    place = lax.broadcasted_iota(jnp.int32, (RANK, RANK), 0)
    source = lax.broadcasted_iota(jnp.int32, (RANK, RANK), 1)
    half, near, far = place // 16, (place // FAR) % NEAR, place % FAR
    wanted = (far * NEAR + near) * 2 + (core + half) % 2
    chosen = nn((source == wanted).astype(F32), factor_ref[...])
    high = chosen.astype(BF16)
    low = (chosen - high.astype(F32)).astype(BF16)
    both = jnp.concatenate([high, low], axis=0)
    dims = (((1,), (1,)), ((), ()))
    for k in range(depth):
        piece = tensor_ref[k]
        piece_high = piece.astype(BF16)
        piece_low = (piece - piece_high.astype(F32)).astype(BF16)
        first = lax.dot_general(both, piece_high, dims, preferred_element_type=F32)
        second = lax.dot_general(high, piece_low, dims, preferred_element_type=F32)
        value = first[:RANK] + first[RANK:] + second
        at = pl.program_id(0) * depth + k
        left_ref[pl.ds(at, RANK, stride=RANK), :] = value[:, :128]
        right_ref[pl.ds(at, RANK, stride=RANK), :] = value[:, 128:]

    @pl.when(pl.program_id(0) == pl.num_programs(0) - 1)
    def _():
        for q, part_ref in enumerate((left_ref, right_ref)):
            keep_ref[:, 128 * q : 128 * q + 128] = part_ref[: 16 * RANK, :]
            send_ref[:, 128 * q : 128 * q + 128] = part_ref[16 * RANK :, :]


def contract(core, factor_two_t, tensor):
    depth = 4
    return pl.pallas_call(
        contract_kernel,
        grid=(RANK // depth,),
        in_specs=[
            pl.BlockSpec(memory_space=pltpu.SMEM),
            pl.BlockSpec((RANK, COLS), lambda g: (0, 0)),
            pl.BlockSpec((depth, ROWS, COLS), lambda g: (g, 0, 0)),
        ],
        out_specs=[pl.BlockSpec((16 * RANK, ROWS), lambda g: (0, 0))] * 2,
        out_shape=[jax.ShapeDtypeStruct((16 * RANK, ROWS), F32)] * 2,
        scratch_shapes=[pltpu.VMEM((RANK * RANK, 128), F32)] * 2,
        name="contract",
    )(core, factor_two_t, tensor)


def call(kernel, outs, *args):
    return pl.pallas_call(
        kernel,
        in_specs=[pl.BlockSpec(memory_space=pltpu.VMEM)] * len(args),
        out_specs=[pl.BlockSpec(memory_space=pltpu.VMEM)] * len(outs),
        out_shape=[jax.ShapeDtypeStruct(shape, F32) for shape in outs],
        name=kernel.__name__,
    )(*args)


def start_kernel(parts_ref, old_ref, own_ref, out_ref):
    own = jnp.sum(parts_ref[...], axis=0)
    own_ref[...] = own
    packed = pack(nt(old_ref[...], own))
    for q in range(16):
        out_ref[q] = packed


def weigh_kernel(parts_ref, three_ref, own_ref, out_ref):
    summed = unpack(jnp.sum(parts_ref[...], axis=0))
    three = three_ref[...]
    weighed = nt(nn(summed, three), three)
    payload = jnp.concatenate([own_ref[...], widen(pack(weighed))], axis=0)
    for q in range(FAR):
        out_ref[q] = payload


def block(mine_ref, other_ref):
    return jnp.concatenate(
        [mine_ref[:, :RANK, :].reshape(FAR * RANK, ROWS), other_ref[:, :RANK, :].reshape(FAR * RANK, ROWS)], axis=0
    )


def image_kernel(mine_ref, other_ref, out_ref):
    weights = jnp.concatenate(
        [unpack(ref[q, RANK : RANK + 8, :128]) for ref in (mine_ref, other_ref) for q in range(FAR)], axis=1
    )
    image = nn(weights, block(mine_ref, other_ref))
    for q in range(NEAR):
        out_ref[q] = image


def project_kernel(parts_ref, mine_ref, other_ref, out_ref):
    image = jnp.sum(parts_ref[...], axis=0)
    out = jnp.concatenate([nt(image, block(mine_ref, other_ref)), widen(pack(nt(image, image)))], axis=0)
    for q in range(16):
        out_ref[q] = out


def step_kernel(parts_ref, three_ref, mine_ref, other_ref, out_ref):
    summed = jnp.sum(parts_ref[...], axis=0)
    (coeffs,) = lower_solve(unpack(summed[RANK:, :128]), [summed[:RANK]])
    three = three_ref[...]
    mixing = nt(three, three)
    tiled = jnp.concatenate([jnp.concatenate([mixing] * 8, axis=0)] * 8, axis=1)
    left = lax.broadcasted_iota(jnp.int32, tiled.shape, 0) // RANK
    right = lax.broadcasted_iota(jnp.int32, tiled.shape, 1) // RANK
    weights = nn(coeffs, jnp.where(left == right, tiled, 0.0))
    image = nn(weights, block(mine_ref, other_ref))
    for q in range(NEAR):
        out_ref[q] = image


def last_kernel(parts_ref, own_ref, image_ref, out_ref):
    image = jnp.sum(parts_ref[...], axis=0)
    image_ref[...] = image
    out = jnp.concatenate([pack(nt(image, own_ref[...])), pack(nt(image, image))], axis=0)
    for q in range(16):
        out_ref[q] = out


def finish_kernel(parts_ref, image_ref, three_ref, factor_ref, core_ref):
    summed = jnp.sum(parts_ref[...], axis=0)
    factor, coeffs = lower_solve(unpack(summed[8:]), [image_ref[...], unpack(summed[:8])])
    factor_ref[...] = factor * math.sqrt(I1)
    core_ref[...] = nn(coeffs, three_ref[...])


def groups(of):
    found = {}
    for z in range(FAR * NEAR):
        for core in range(2):
            found.setdefault(of(z // NEAR, z % NEAR, core), []).append(z * 2 + core)
    return list(found.values())


NEAR_GROUPS = groups(lambda far, near, core: (far, core))
FAR_GROUPS = groups(lambda far, near, core: (near, core))
PAIRS = [(c, c ^ 1) for c in range(32)]


def exchange(values, axis, index_groups=None):
    return lax.all_to_all(values, axis, 0, 0, axis_index_groups=index_groups)


def shards(tensor, old_factor, factor_two, factor_three):
    core = (lax.axis_index("col") % 2).astype(jnp.int32).reshape(1)
    keep, send = contract(core, factor_two.T, tensor)
    partial_value = keep + lax.ppermute(send, "col", PAIRS)
    partial_value = exchange(partial_value.reshape(NEAR, FAR * RANK, ROWS), "col", NEAR_GROUPS)
    partial_value = jnp.sum(partial_value, axis=0).reshape(FAR, RANK, ROWS)
    parts = exchange(partial_value, "col", FAR_GROUPS)
    own, parts = call(start_kernel, [(RANK, ROWS), (16, 8, 128)], parts, old_factor.T)
    parts = exchange(parts, "row")
    (parts,) = call(weigh_kernel, [(FAR, RANK + 8, ROWS)], parts, factor_three, own)
    mine = exchange(parts, "col", FAR_GROUPS)
    other = lax.ppermute(mine, "col", PAIRS)
    (parts,) = call(image_kernel, [(NEAR, RANK, ROWS)], mine, other)
    parts = exchange(parts, "col", NEAR_GROUPS)
    (parts,) = call(project_kernel, [(16, RANK + 8, ROWS)], parts, mine, other)
    parts = exchange(parts, "row")
    (parts,) = call(step_kernel, [(NEAR, RANK, ROWS)], parts, factor_three, mine, other)
    parts = exchange(parts, "col", NEAR_GROUPS)
    image, parts = call(last_kernel, [(RANK, ROWS), (16, 16, 128)], parts, own)
    parts = exchange(parts, "row")
    factor, core_part = call(finish_kernel, [(RANK, ROWS), (RANK, RANK)], parts, image, factor_three)
    return factor.T, core_part


def solution(mesh):
    return jax.shard_map(
        shards,
        mesh=mesh,
        in_specs=(P(None, "row", "col"), P("row", None), P("col", None), P()),
        out_specs=(P("row", None), P(None, "col")),
        check_vma=False,
    )
```

```python
import math

import jax
import jax.numpy as jnp
from jax import lax
from jax.experimental import pallas as pl
from jax.experimental.pallas import tpu as pltpu
from jax.sharding import PartitionSpec as P

I1 = 4096
RANK = 32
NEAR = 4
FAR = 4
GROUP = 2 * NEAR
ROWS = 256
COLS = 128
PANEL = 4
HIGHEST = lax.Precision.HIGHEST
F32 = jnp.float32
BF16 = jnp.bfloat16


def nn(a, b):
    return lax.dot_general(a, b, (((1,), (0,)), ((), ())), precision=HIGHEST, preferred_element_type=F32)


def nt(a, b):
    return lax.dot_general(a, b, (((1,), (1,)), ((), ())), precision=HIGHEST, preferred_element_type=F32)


def pack(square):
    return jnp.concatenate([square[8 * q : 8 * q + 8] for q in range(4)], axis=1)


def unpack(packed):
    return jnp.concatenate([packed[:, 32 * q : 32 * q + 32] for q in range(4)], axis=0)


def lower_solve(gram, sides):
    arrays = [jnp.concatenate([gram, jnp.zeros((RANK, 128 - RANK), F32)], axis=1), *sides]
    row_of = lax.broadcasted_iota(jnp.int32, (RANK, 128), 0)
    diagonal = jnp.zeros((RANK, 128), F32)
    for j in range(0, RANK, PANEL):
        columns = [jnp.broadcast_to(arrays[0][:, j + p : j + p + 1], (RANK, 128)) for p in range(PANEL)]
        factors = []
        for p in range(PANEL):
            pivot = columns[p][j + p : j + p + 1]
            diagonal = jnp.where(row_of == j + p, pivot, diagonal)
            factors.append(jnp.where(row_of > j + p, columns[p], 0.0) * (1.0 / pivot))
            for q in range(p + 1, PANEL):
                columns[q] = columns[q] - factors[p] * columns[q][j + p : j + p + 1]
        updated = []
        for array in arrays:
            rows = []
            for p in range(PANEL):
                row = array[j + p : j + p + 1]
                for q in range(p):
                    row = row - factors[q][j + p : j + p + 1] * rows[q]
                rows.append(row)
            for p in range(PANEL):
                array = array - factors[p] * rows[p]
            updated.append(array)
        arrays = updated
    scale = lax.rsqrt(diagonal)
    return [array * scale for array in arrays[1:]]


def contract_kernel(core_ref, factor_ref, tensor_ref, keep_ref, send_ref, left_ref, right_ref):
    depth = tensor_ref.shape[0]
    core = core_ref[0]
    place = lax.broadcasted_iota(jnp.int32, (RANK, RANK), 0)
    source = lax.broadcasted_iota(jnp.int32, (RANK, RANK), 1)
    half, near, far = place // 16, (place // FAR) % NEAR, place % FAR
    wanted = (far * NEAR + near) * 2 + (core + half) % 2
    chosen = nn((source == wanted).astype(F32), factor_ref[...])
    high = chosen.astype(BF16)
    low = (chosen - high.astype(F32)).astype(BF16)
    weights = jnp.concatenate([jnp.concatenate([part, part], axis=1) for part in (high, low)], axis=0)
    for k in range(depth):
        piece = tensor_ref[k]
        piece_high = piece.astype(BF16)
        piece_low = (piece - piece_high.astype(F32)).astype(BF16)
        pieces = jnp.concatenate([piece_high, piece_low], axis=1)
        both = lax.dot_general(weights, pieces, (((1,), (1,)), ((), ())), preferred_element_type=F32)
        value = both[:RANK] + both[RANK:]
        at = pl.program_id(0) * depth + k
        left_ref[pl.ds(at, RANK, stride=RANK), :] = value[:, :128]
        right_ref[pl.ds(at, RANK, stride=RANK), :] = value[:, 128:]

    @pl.when(pl.program_id(0) == pl.num_programs(0) - 1)
    def _():
        for q, part_ref in enumerate((left_ref, right_ref)):
            keep_ref[:, 128 * q : 128 * q + 128] = part_ref[: 16 * RANK, :]
            send_ref[:, 128 * q : 128 * q + 128] = part_ref[16 * RANK :, :]


def contract(core, factor_two_t, tensor):
    depth = 16
    return pl.pallas_call(
        contract_kernel,
        grid=(RANK // depth,),
        in_specs=[
            pl.BlockSpec(memory_space=pltpu.SMEM),
            pl.BlockSpec((RANK, COLS), lambda g: (0, 0)),
            pl.BlockSpec((depth, ROWS, COLS), lambda g: (g, 0, 0)),
        ],
        out_specs=[pl.BlockSpec(memory_space=pltpu.VMEM)] * 2,
        out_shape=[pltpu.VMEM((16 * RANK, ROWS), F32)] * 2,
        scratch_shapes=[pltpu.VMEM((RANK * RANK, 128), F32)] * 2,
        name="contract",
    )(core, factor_two_t, tensor)


def call(kernel, outs, *args, place=pltpu.VMEM):
    return pl.pallas_call(
        kernel,
        in_specs=[pl.BlockSpec(memory_space=pltpu.VMEM)] * len(args),
        out_specs=[pl.BlockSpec(memory_space=pltpu.VMEM)] * len(outs),
        out_shape=[place(shape, F32) for shape in outs],
        name=kernel.__name__,
    )(*[pltpu.with_memory_space_constraint(arg, pltpu.VMEM) for arg in args])


def start_kernel(parts_ref, old_ref, own_ref, out_ref):
    own = jnp.sum(parts_ref[...], axis=0)
    own_ref[...] = own
    packed = pack(nt(old_ref[...], own))
    for q in range(16):
        out_ref[q] = packed


def weigh_kernel(parts_ref, three_ref, own_ref, out_ref):
    summed = unpack(jnp.sum(parts_ref[...], axis=0))
    three = three_ref[...]
    packed = pack(nt(nn(summed, three), three))
    packed = jnp.concatenate([packed, jnp.zeros_like(packed)], axis=1)
    payload = jnp.concatenate([own_ref[...], packed], axis=0)
    for q in range(FAR):
        out_ref[q] = payload


def block(held_ref):
    return held_ref[:, :RANK, :].reshape(FAR * RANK, ROWS)


def image_kernel(held_ref, out_ref):
    weights = jnp.concatenate([unpack(held_ref[q, RANK : RANK + 8, :128]) for q in range(FAR)], axis=1)
    image = nn(weights, block(held_ref))
    for q in range(GROUP):
        out_ref[q] = image


def project_kernel(parts_ref, held_ref, out_ref):
    image = jnp.sum(parts_ref[...], axis=0)
    out = jnp.concatenate([nt(image, block(held_ref)), pack(nt(image, image))], axis=0)
    for q in range(16):
        out_ref[q] = out


def step_kernel(parts_ref, three_ref, held_ref, out_ref):
    summed = jnp.sum(parts_ref[...], axis=0)
    (coeffs,) = lower_solve(unpack(summed[RANK:]), [summed[:RANK]])
    three = three_ref[...]
    mixing = nt(three, three)
    tiled = jnp.concatenate([jnp.concatenate([mixing] * FAR, axis=0)] * FAR, axis=1)
    left = lax.broadcasted_iota(jnp.int32, tiled.shape, 0) // RANK
    right = lax.broadcasted_iota(jnp.int32, tiled.shape, 1) // RANK
    weights = nn(coeffs, jnp.where(left == right, tiled, 0.0))
    image = nn(weights, block(held_ref))
    for q in range(GROUP):
        out_ref[q] = image


def last_kernel(parts_ref, own_ref, image_ref, out_ref):
    image = jnp.sum(parts_ref[...], axis=0)
    image_ref[...] = image
    out = jnp.concatenate([pack(nt(image, own_ref[...])), pack(nt(image, image))], axis=0)
    for q in range(16):
        out_ref[q] = out


def finish_kernel(parts_ref, image_ref, three_ref, factor_ref, core_ref):
    summed = jnp.sum(parts_ref[...], axis=0)
    coeffs = jnp.concatenate([unpack(summed[:8]), jnp.zeros((RANK, 128 - RANK), F32)], axis=1)
    left, right, coeffs = lower_solve(unpack(summed[8:]), [image_ref[:, :128], image_ref[:, 128:], coeffs])
    factor_ref[:, :128] = left * math.sqrt(I1)
    factor_ref[:, 128:] = right * math.sqrt(I1)
    core_ref[...] = nn(coeffs[:, :RANK], three_ref[...])


def groups(of):
    found = {}
    for z in range(FAR * NEAR):
        for core in range(2):
            found.setdefault(of(z // NEAR, z % NEAR, core), []).append(z * 2 + core)
    return list(found.values())


NEAR_GROUPS = groups(lambda far, near, core: (far, core))
FAR_GROUPS = groups(lambda far, near, core: (near, core))
BLOCK_GROUPS = groups(lambda far, near, core: far)
PAIRS = [(c, c ^ 1) for c in range(32)]


def exchange(values, axis, index_groups=None):
    return lax.all_to_all(values, axis, 0, 0, axis_index_groups=index_groups)


def shards(tensor, old_factor, factor_two, factor_three):
    core = (lax.axis_index("col") & 1).astype(jnp.int32).reshape(1)
    keep, send = contract(core, factor_two.T, tensor)
    partial_value = keep + lax.ppermute(send, "col", PAIRS)
    partial_value = exchange(partial_value.reshape(NEAR, FAR * RANK, ROWS), "col", NEAR_GROUPS)
    partial_value = jnp.sum(partial_value, axis=0).reshape(FAR, RANK, ROWS)
    parts = exchange(partial_value, "col", FAR_GROUPS)
    own, parts = call(start_kernel, [(RANK, ROWS), (16, 8, 128)], parts, old_factor.T)
    parts = exchange(parts, "row")
    (parts,) = call(weigh_kernel, [(FAR, RANK + 8, ROWS)], parts, factor_three, own)
    held = exchange(parts, "col", FAR_GROUPS)
    (parts,) = call(image_kernel, [(GROUP, RANK, ROWS)], held)
    parts = exchange(parts, "col", BLOCK_GROUPS)
    (parts,) = call(project_kernel, [(16, RANK + 8, 128)], parts, held)
    parts = exchange(parts, "row")
    (parts,) = call(step_kernel, [(GROUP, RANK, ROWS)], parts, factor_three, held)
    parts = exchange(parts, "col", BLOCK_GROUPS)
    image, parts = call(last_kernel, [(RANK, ROWS), (16, 16, 128)], parts, own)
    parts = exchange(parts, "row")
    outs = [(RANK, ROWS), (RANK, RANK)]
    factor, core_part = call(finish_kernel, outs, parts, image, factor_three, place=jax.ShapeDtypeStruct)
    return factor.T, core_part


def solution(mesh):
    return jax.shard_map(
        shards,
        mesh=mesh,
        in_specs=(P(None, "row", "col"), P("row", None), P("col", None), P()),
        out_specs=(P("row", None), P(None, "col")),
        check_vma=False,
    )
```

```python
import math

import jax
import jax.numpy as jnp
from jax import lax
from jax.experimental import pallas as pl
from jax.experimental.pallas import tpu as pltpu
from jax.sharding import PartitionSpec as P

I1 = 4096
RANK = 32
NEAR = 4
FAR = 4
PIECES = (8, 12, 12)
ROWS = 256
COLS = 128
PANEL = 8
HIGHEST = lax.Precision.HIGHEST
F32 = jnp.float32
BF16 = jnp.bfloat16


def nn(a, b):
    return lax.dot_general(a, b, (((1,), (0,)), ((), ())), precision=HIGHEST, preferred_element_type=F32)


def nt(a, b):
    return lax.dot_general(a, b, (((1,), (1,)), ((), ())), precision=HIGHEST, preferred_element_type=F32)


def pack(square):
    return jnp.concatenate([square[8 * q : 8 * q + 8] for q in range(4)], axis=1)


def unpack(packed):
    return jnp.concatenate([packed[:, 32 * q : 32 * q + 32] for q in range(4)], axis=0)


def lower_solve(gram, sides):
    arrays = [jnp.concatenate([gram, jnp.zeros((RANK, 128 - RANK), F32)], axis=1), *sides]
    row_of = lax.broadcasted_iota(jnp.int32, (RANK, 128), 0)
    diagonal = jnp.zeros((RANK, 128), F32)
    for j in range(0, RANK, PANEL):
        columns = [jnp.broadcast_to(arrays[0][:, j + p : j + p + 1], (RANK, 128)) for p in range(PANEL)]
        factors = []
        for p in range(PANEL):
            pivot = columns[p][j + p : j + p + 1]
            diagonal = jnp.where(row_of == j + p, pivot, diagonal)
            factors.append(jnp.where(row_of > j + p, columns[p], 0.0) * (1.0 / pivot))
            for q in range(p + 1, PANEL):
                columns[q] = columns[q] - factors[p] * columns[q][j + p : j + p + 1]
        updated = []
        for array in arrays:
            rows = []
            for p in range(PANEL):
                row = array[j + p : j + p + 1]
                for q in range(p):
                    row = row - factors[q][j + p : j + p + 1] * rows[q]
                rows.append(row)
            for p in range(PANEL):
                array = array - factors[p] * rows[p]
            updated.append(array)
        arrays = updated
    scale = lax.rsqrt(diagonal)
    return [array * scale for array in arrays[1:]]


def split(value):
    high = value.astype(BF16)
    return high, (value - high.astype(F32)).astype(BF16)


def contract_kernel(
    core_ref, factor_ref, tensor_ref, keep_ref, send_ref, left_ref, right_ref, two_ref, held_ref, arrived
):
    first = pltpu.make_async_copy(factor_ref, two_ref, arrived.at[len(PIECES)])
    first.start()
    starts = [sum(PIECES[:p]) for p in range(len(PIECES))]
    copies = [
        pltpu.make_async_copy(tensor_ref.at[pl.ds(start, size)], held_ref.at[pl.ds(start, size)], arrived.at[p])
        for p, (start, size) in enumerate(zip(starts, PIECES))
    ]
    for copy in copies:
        copy.start()
    place = lax.broadcasted_iota(jnp.int32, (RANK, RANK), 0)
    source = lax.broadcasted_iota(jnp.int32, (RANK, RANK), 1)
    near, far = (place // FAR) % NEAR, place % FAR
    core = (core_ref[0] + place // 16) % 2
    wanted = (far * NEAR + (near + far) % NEAR) * 2 + core
    first.wait()
    high, low = split(nn((source == wanted).astype(F32), two_ref[...]))
    weights = jnp.concatenate([jnp.concatenate([part, part], axis=1) for part in (high, low)], axis=0)
    for copy, start, size in zip(copies, starts, PIECES):
        copy.wait()
        for k in range(start, start + size):
            pieces = jnp.concatenate(split(held_ref[k]), axis=1)
            both = lax.dot_general(weights, pieces, (((1,), (1,)), ((), ())), preferred_element_type=F32)
            value = both[:RANK] + both[RANK:]
            left_ref[pl.ds(k, RANK, stride=RANK), :] = value[:, :128]
            right_ref[pl.ds(k, RANK, stride=RANK), :] = value[:, 128:]
    for q, part_ref in enumerate((left_ref, right_ref)):
        keep_ref[:, 128 * q : 128 * q + 128] = part_ref[: 16 * RANK, :]
        send_ref[:, 128 * q : 128 * q + 128] = part_ref[16 * RANK :, :]


def contract(core, factor_two_t, tensor):
    return pl.pallas_call(
        contract_kernel,
        in_specs=[
            pl.BlockSpec(memory_space=pltpu.SMEM),
            pl.BlockSpec(memory_space=pltpu.HBM),
            pl.BlockSpec(memory_space=pltpu.HBM),
        ],
        out_specs=[pl.BlockSpec(memory_space=pltpu.VMEM)] * 2,
        out_shape=[pltpu.VMEM((16 * RANK, ROWS), F32)] * 2,
        scratch_shapes=[
            pltpu.VMEM((RANK * RANK, 128), F32),
            pltpu.VMEM((RANK * RANK, 128), F32),
            pltpu.VMEM((RANK, COLS), F32),
            pltpu.VMEM((RANK, ROWS, COLS), F32),
            pltpu.SemaphoreType.DMA((len(PIECES) + 1,)),
        ],
        name="contract",
    )(core, factor_two_t, tensor)


def call(kernel, outs, *args, place=pltpu.VMEM):
    return pl.pallas_call(
        kernel,
        in_specs=[pl.BlockSpec(memory_space=pltpu.VMEM)] * len(args),
        out_specs=[pl.BlockSpec(memory_space=pltpu.VMEM)] * len(outs),
        out_shape=[place(shape, F32) for shape in outs],
        name=kernel.__name__,
    )(*[pltpu.with_memory_space_constraint(arg, pltpu.VMEM) for arg in args])


def total_kernel(parts_ref, out_ref):
    out_ref[...] = jnp.sum(parts_ref[...], axis=0)


def start_kernel(parts_ref, old_ref, own_ref, out_ref):
    own = jnp.sum(parts_ref[...], axis=0)
    own_ref[...] = own
    packed = pack(nt(old_ref[...], own))
    for q in range(16):
        out_ref[q] = packed


def weigh_kernel(parts_ref, three_ref, own_ref, out_ref):
    summed = unpack(jnp.sum(parts_ref[...], axis=0))
    three = three_ref[...]
    payload = jnp.concatenate([own_ref[:, :128], own_ref[:, 128:], pack(nt(nn(summed, three), three))], axis=0)
    for q in range(FAR):
        out_ref[q] = payload


def block(*held):
    rows = [jnp.concatenate([ref[q, :RANK], ref[q, RANK : 2 * RANK]], axis=1) for ref in held for q in range(FAR)]
    return jnp.concatenate(rows, axis=0)


def image_kernel(mine_ref, other_ref, out_ref):
    weights = [unpack(ref[q, 2 * RANK :]) for ref in (mine_ref, other_ref) for q in range(FAR)]
    image = nn(jnp.concatenate(weights, axis=1), block(mine_ref, other_ref))
    for q in range(NEAR):
        out_ref[q] = image


def project_kernel(parts_ref, mine_ref, other_ref, out_ref):
    image = jnp.sum(parts_ref[...], axis=0)
    projected = nt(image, block(mine_ref, other_ref))
    out = jnp.concatenate([projected[:, :128], projected[:, 128:], pack(nt(image, image))], axis=0)
    for q in range(16):
        out_ref[q] = out


def step_kernel(parts_ref, three_ref, mine_ref, other_ref, out_ref):
    summed = jnp.sum(parts_ref[...], axis=0)
    sides = lower_solve(unpack(summed[2 * RANK :]), [summed[:RANK], summed[RANK : 2 * RANK]])
    three = three_ref[...]
    mixing = nt(three, three)
    tiled = jnp.concatenate([jnp.concatenate([mixing] * FAR, axis=0)] * FAR, axis=1)
    left = lax.broadcasted_iota(jnp.int32, tiled.shape, 0) // RANK
    right = lax.broadcasted_iota(jnp.int32, tiled.shape, 1) // RANK
    mixing = jnp.where(left == right, tiled, 0.0)
    weights = jnp.concatenate([nn(side, mixing) for side in sides], axis=1)
    image = nn(weights, block(mine_ref, other_ref))
    for q in range(NEAR):
        out_ref[q] = image


def last_kernel(parts_ref, own_ref, image_ref, out_ref):
    image = jnp.sum(parts_ref[...], axis=0)
    image_ref[...] = image
    out = jnp.concatenate([pack(nt(image, own_ref[...])), pack(nt(image, image))], axis=0)
    for q in range(16):
        out_ref[q] = out


def finish_kernel(parts_ref, image_ref, three_ref, factor_ref, core_ref):
    summed = jnp.sum(parts_ref[...], axis=0)
    coeffs = jnp.concatenate([unpack(summed[:8]), jnp.zeros((RANK, 128 - RANK), F32)], axis=1)
    left, right, coeffs = lower_solve(unpack(summed[8:]), [image_ref[:, :128], image_ref[:, 128:], coeffs])
    factor_ref[:, :128] = left * math.sqrt(I1)
    factor_ref[:, 128:] = right * math.sqrt(I1)
    core_ref[...] = nn(coeffs[:, :RANK], three_ref[...])


def groups(by_far):
    found = [[] for _ in range(2 * FAR * NEAR // (FAR if by_far else NEAR))]
    for core in range(2):
        for far in range(FAR):
            for near in range(NEAR):
                chip = far * NEAR + (near + far) % NEAR
                found[(near if by_far else far) * 2 + core].append(chip * 2 + core)
    return found


NEAR_GROUPS = groups(by_far=False)
FAR_GROUPS = groups(by_far=True)
PAIRS = [(c, c ^ 1) for c in range(32)]


def exchange(values, axis, index_groups=None):
    return lax.all_to_all(values, axis, 0, 0, axis_index_groups=index_groups)


def shards(tensor, old_factor, factor_two, factor_three):
    core = (lax.axis_index("col") & 1).astype(jnp.int32).reshape(1)
    keep, send = contract(core, factor_two.T, tensor)
    value = keep + lax.ppermute(send, "col", PAIRS)
    parts = exchange(value.reshape(NEAR, FAR * RANK, ROWS), "col", NEAR_GROUPS)
    (value,) = call(total_kernel, [(FAR * RANK, ROWS)], parts)
    parts = exchange(value.reshape(FAR, RANK, ROWS), "col", FAR_GROUPS)
    own, parts = call(start_kernel, [(RANK, ROWS), (16, 8, 128)], parts, old_factor.T)
    parts = exchange(parts, "row")
    (parts,) = call(weigh_kernel, [(FAR, 2 * RANK + 8, 128)], parts, factor_three, own)
    mine = exchange(parts, "col", FAR_GROUPS)
    other = lax.ppermute(mine, "col", PAIRS)
    (parts,) = call(image_kernel, [(NEAR, RANK, ROWS)], mine, other)
    parts = exchange(parts, "col", NEAR_GROUPS)
    (parts,) = call(project_kernel, [(16, 2 * RANK + 8, 128)], parts, mine, other)
    parts = exchange(parts, "row")
    (parts,) = call(step_kernel, [(NEAR, RANK, ROWS)], parts, factor_three, mine, other)
    parts = exchange(parts, "col", NEAR_GROUPS)
    image, parts = call(last_kernel, [(RANK, ROWS), (16, 16, 128)], parts, own)
    parts = exchange(parts, "row")
    outs = [(RANK, ROWS), (RANK, RANK)]
    factor, core_part = call(finish_kernel, outs, parts, image, factor_three, place=jax.ShapeDtypeStruct)
    return factor.T, core_part


def solution(mesh):
    return jax.shard_map(
        shards,
        mesh=mesh,
        in_specs=(P(None, "row", "col"), P("row", None), P("col", None), P()),
        out_specs=(P("row", None), P(None, "col")),
        check_vma=False,
    )
```

```python
import math

import jax
import jax.numpy as jnp
from jax import lax
from jax.experimental import pallas as pl
from jax.experimental.pallas import tpu as pltpu
from jax.sharding import PartitionSpec as P

I1 = 4096
RANK = 32
NEAR = 4
FAR = 4
PIECES = (8, 12, 12)
ROWS = 256
COLS = 128
PANEL = 8
SHIFT = 2
HIGHEST = lax.Precision.HIGHEST
F32 = jnp.float32
BF16 = jnp.bfloat16


def nn(a, b):
    return lax.dot_general(a, b, (((1,), (0,)), ((), ())), precision=HIGHEST, preferred_element_type=F32)


def nt(a, b):
    return lax.dot_general(a, b, (((1,), (1,)), ((), ())), precision=HIGHEST, preferred_element_type=F32)


def pack(square):
    return jnp.concatenate([square[8 * q : 8 * q + 8] for q in range(4)], axis=1)


def unpack(packed):
    return jnp.concatenate([packed[:, 32 * q : 32 * q + 32] for q in range(4)], axis=0)


def lower_solve(gram, sides):
    arrays = [jnp.concatenate([gram, jnp.zeros((RANK, 128 - RANK), F32)], axis=1), *sides]
    row_of = lax.broadcasted_iota(jnp.int32, (RANK, 128), 0)
    diagonal = jnp.zeros((RANK, 128), F32)
    for j in range(0, RANK, PANEL):
        columns = [jnp.broadcast_to(arrays[0][:, j + p : j + p + 1], (RANK, 128)) for p in range(PANEL)]
        factors = []
        for p in range(PANEL):
            pivot = columns[p][j + p : j + p + 1]
            diagonal = jnp.where(row_of == j + p, pivot, diagonal)
            factors.append(jnp.where(row_of > j + p, columns[p], 0.0) * (1.0 / pivot))
            for q in range(p + 1, PANEL):
                columns[q] = columns[q] - factors[p] * columns[q][j + p : j + p + 1]
        updated = []
        for array in arrays:
            rows = []
            for p in range(PANEL):
                row = array[j + p : j + p + 1]
                for q in range(p):
                    row = row - factors[q][j + p : j + p + 1] * rows[q]
                rows.append(row)
            for p in range(PANEL):
                array = array - factors[p] * rows[p]
            updated.append(array)
        arrays = updated
    scale = lax.rsqrt(diagonal)
    return [array * scale for array in arrays[1:]]


def split(value):
    high = value.astype(BF16)
    return high, (value - high.astype(F32)).astype(BF16)


def contract_kernel(
    core_ref, factor_ref, tensor_ref, keep_ref, send_ref, left_ref, right_ref, two_ref, held_ref, arrived
):
    first = pltpu.make_async_copy(factor_ref, two_ref, arrived.at[len(PIECES)])
    first.start()
    starts = [sum(PIECES[:p]) for p in range(len(PIECES))]
    copies = [
        pltpu.make_async_copy(tensor_ref.at[pl.ds(start, size)], held_ref.at[pl.ds(start, size)], arrived.at[p])
        for p, (start, size) in enumerate(zip(starts, PIECES))
    ]
    for copy in copies:
        copy.start()
    place = lax.broadcasted_iota(jnp.int32, (RANK, RANK), 0)
    source = lax.broadcasted_iota(jnp.int32, (RANK, RANK), 1)
    near, far = (place // FAR) % NEAR, place % FAR
    core = (core_ref[0] + place // 16) % 2
    wanted = (far * NEAR + (near + far) % NEAR + SHIFT * core) % (FAR * NEAR) * 2 + core
    first.wait()
    high, low = split(nn((source == wanted).astype(F32), two_ref[...]))
    weights = jnp.concatenate([jnp.concatenate([part, part], axis=1) for part in (high, low)], axis=0)
    for copy, start, size in zip(copies, starts, PIECES):
        copy.wait()
        for k in range(start, start + size):
            pieces = jnp.concatenate(split(held_ref[k]), axis=1)
            both = lax.dot_general(weights, pieces, (((1,), (1,)), ((), ())), preferred_element_type=F32)
            value = both[:RANK] + both[RANK:]
            left_ref[pl.ds(k, RANK, stride=RANK), :] = value[:, :128]
            right_ref[pl.ds(k, RANK, stride=RANK), :] = value[:, 128:]
    for q, part_ref in enumerate((left_ref, right_ref)):
        keep_ref[:, 128 * q : 128 * q + 128] = part_ref[: 16 * RANK, :]
        send_ref[:, 128 * q : 128 * q + 128] = part_ref[16 * RANK :, :]


def contract(core, factor_two_t, tensor):
    return pl.pallas_call(
        contract_kernel,
        in_specs=[
            pl.BlockSpec(memory_space=pltpu.SMEM),
            pl.BlockSpec(memory_space=pltpu.HBM),
            pl.BlockSpec(memory_space=pltpu.HBM),
        ],
        out_specs=[pl.BlockSpec(memory_space=pltpu.VMEM)] * 2,
        out_shape=[pltpu.VMEM((16 * RANK, ROWS), F32)] * 2,
        scratch_shapes=[
            pltpu.VMEM((RANK * RANK, 128), F32),
            pltpu.VMEM((RANK * RANK, 128), F32),
            pltpu.VMEM((RANK, COLS), F32),
            pltpu.VMEM((RANK, ROWS, COLS), F32),
            pltpu.SemaphoreType.DMA((len(PIECES) + 1,)),
        ],
        name="contract",
    )(core, factor_two_t, tensor)


def call(kernel, outs, *args, place=pltpu.VMEM):
    return pl.pallas_call(
        kernel,
        in_specs=[pl.BlockSpec(memory_space=pltpu.VMEM)] * len(args),
        out_specs=[pl.BlockSpec(memory_space=pltpu.VMEM)] * len(outs),
        out_shape=[place(shape, F32) for shape in outs],
        name=kernel.__name__,
    )(*[pltpu.with_memory_space_constraint(arg, pltpu.VMEM) for arg in args])


def total_kernel(parts_ref, out_ref):
    out_ref[...] = jnp.sum(parts_ref[...], axis=0)


def start_kernel(parts_ref, old_ref, own_ref, out_ref):
    own = jnp.sum(parts_ref[...], axis=0)
    own_ref[...] = own
    packed = pack(nt(old_ref[...], own))
    for q in range(16):
        out_ref[q] = packed


def weigh_kernel(parts_ref, three_ref, own_ref, out_ref):
    summed = unpack(jnp.sum(parts_ref[...], axis=0))
    three = three_ref[...]
    payload = jnp.concatenate([own_ref[:, :128], own_ref[:, 128:], pack(nt(nn(summed, three), three))], axis=0)
    for q in range(FAR):
        out_ref[q] = payload


def block(held):
    sides = [held[h, q] for h in range(2) for q in range(FAR)]
    rows = [jnp.concatenate([side[:RANK], side[RANK : 2 * RANK]], axis=1) for side in sides]
    return jnp.concatenate(rows, axis=0)


def image_kernel(held_ref, out_ref):
    weights = [unpack(held_ref[h, q, 2 * RANK :]) for h in range(2) for q in range(FAR)]
    image = nn(jnp.concatenate(weights, axis=1), block(held_ref))
    for q in range(NEAR):
        out_ref[q] = image


def project_kernel(parts_ref, held_ref, out_ref):
    image = jnp.sum(parts_ref[...], axis=0)
    projected = nt(image, block(held_ref))
    out = jnp.concatenate([projected[:, :128], projected[:, 128:], pack(nt(image, image))], axis=0)
    for q in range(16):
        out_ref[q] = out


def step_kernel(parts_ref, three_ref, held_ref, out_ref):
    summed = jnp.sum(parts_ref[...], axis=0)
    three = three_ref[...]
    mixing = nt(three, three)
    tiled = jnp.concatenate([jnp.concatenate([mixing] * FAR, axis=0)] * FAR, axis=1)
    left = lax.broadcasted_iota(jnp.int32, tiled.shape, 0) // RANK
    right = lax.broadcasted_iota(jnp.int32, tiled.shape, 1) // RANK
    mixing = jnp.where(left == right, tiled, 0.0)
    weights = [nt(summed[:RANK], mixing), nt(summed[RANK : 2 * RANK], mixing)]
    sides = lower_solve(unpack(summed[2 * RANK :]), weights)
    image = nn(jnp.concatenate(sides, axis=1), block(held_ref))
    for q in range(NEAR):
        out_ref[q] = image


def last_kernel(parts_ref, own_ref, image_ref, out_ref):
    image = jnp.sum(parts_ref[...], axis=0)
    image_ref[...] = image
    out = jnp.concatenate([pack(nt(image, own_ref[...])), pack(nt(image, image))], axis=0)
    for q in range(16):
        out_ref[q] = out


def finish_kernel(parts_ref, image_ref, three_ref, factor_ref, core_ref):
    summed = jnp.sum(parts_ref[...], axis=0)
    coeffs = nn(unpack(summed[:8]), three_ref[...])
    coeffs = jnp.concatenate([coeffs, jnp.zeros((RANK, 128 - RANK), F32)], axis=1)
    left, right, coeffs = lower_solve(unpack(summed[8:]), [image_ref[:, :128], image_ref[:, 128:], coeffs])
    factor_ref[:, :128] = left * math.sqrt(I1)
    factor_ref[:, 128:] = right * math.sqrt(I1)
    core_ref[...] = coeffs[:, :RANK]


def groups(by_far, shift=0):
    found = [[] for _ in range(2 * FAR * NEAR // (FAR if by_far else NEAR))]
    for core in range(2):
        for far in range(FAR):
            for near in range(NEAR):
                chip = (far * NEAR + (near + far) % NEAR + shift * core) % (FAR * NEAR)
                found[(near if by_far else far) * 2 + core].append(chip * 2 + core)
    return found


NEAR_GROUPS = groups(by_far=False)
FAR_GROUPS = groups(by_far=True)
NEAR_SCATTER = groups(by_far=False, shift=SHIFT)
FAR_SCATTER = groups(by_far=True, shift=SHIFT)
CORES = [[c, c + 1] for c in range(0, 32, 2)]
PAIRS = [(c, c ^ 1) for c in range(32)]


def exchange(values, axis, index_groups=None):
    return lax.all_to_all(values, axis, 0, 0, axis_index_groups=index_groups)


def shards(tensor, old_factor, factor_two, factor_three):
    core = (lax.axis_index("col") & 1).astype(jnp.int32).reshape(1)
    keep, send = contract(core, factor_two.T, tensor)
    value = keep + lax.ppermute(send, "col", PAIRS)
    parts = exchange(value.reshape(NEAR, FAR * RANK, ROWS), "col", NEAR_SCATTER)
    (value,) = call(total_kernel, [(FAR * RANK, ROWS)], parts)
    parts = exchange(value.reshape(FAR, RANK, ROWS), "col", FAR_SCATTER)
    own, parts = call(start_kernel, [(RANK, ROWS), (16, 8, 128)], parts, old_factor.T)
    parts = exchange(parts, "row")
    (parts,) = call(weigh_kernel, [(FAR, 2 * RANK + 8, 128)], parts, factor_three, own)
    mine = exchange(parts, "col", FAR_GROUPS)
    held = lax.all_gather(mine, "col", axis_index_groups=CORES)
    (parts,) = call(image_kernel, [(NEAR, RANK, ROWS)], held)
    parts = exchange(parts, "col", NEAR_GROUPS)
    (parts,) = call(project_kernel, [(16, 2 * RANK + 8, 128)], parts, held)
    parts = exchange(parts, "row")
    (parts,) = call(step_kernel, [(NEAR, RANK, ROWS)], parts, factor_three, held)
    parts = exchange(parts, "col", NEAR_GROUPS)
    image, parts = call(last_kernel, [(RANK, ROWS), (16, 16, 128)], parts, own)
    parts = exchange(parts, "row")
    outs = [(RANK, ROWS), (RANK, RANK)]
    factor, core_part = call(finish_kernel, outs, parts, image, factor_three, place=jax.ShapeDtypeStruct)
    return factor.T, core_part


def solution(mesh):
    return jax.shard_map(
        shards,
        mesh=mesh,
        in_specs=(P(None, "row", "col"), P("row", None), P("col", None), P()),
        out_specs=(P("row", None), P(None, "col")),
        check_vma=False,
    )
```

```python
import math

import jax
import jax.numpy as jnp
from jax import lax
from jax.experimental import pallas as pl
from jax.experimental.pallas import tpu as pltpu
from jax.sharding import PartitionSpec as P

I1 = 4096
RANK = 32
NEAR = 4
FAR = 4
PIECES = (8, 12, 12)
ROWS = 256
COLS = 128
PANEL = 8
SHIFT = 2
HIGHEST = lax.Precision.HIGHEST
F32 = jnp.float32
BF16 = jnp.bfloat16


def nn(a, b):
    return lax.dot_general(a, b, (((1,), (0,)), ((), ())), precision=HIGHEST, preferred_element_type=F32)


def nt(a, b):
    return lax.dot_general(a, b, (((1,), (1,)), ((), ())), precision=HIGHEST, preferred_element_type=F32)


def pack(square):
    return jnp.concatenate([square[8 * q : 8 * q + 8] for q in range(4)], axis=1)


def unpack(packed):
    return jnp.concatenate([packed[:, 32 * q : 32 * q + 32] for q in range(4)], axis=0)


def lower_solve(gram, sides):
    arrays = [jnp.concatenate([gram, jnp.zeros((RANK, 128 - RANK), F32)], axis=1), *sides]
    row_of = lax.broadcasted_iota(jnp.int32, (RANK, 128), 0)
    diagonal = jnp.zeros((RANK, 128), F32)
    for j in range(0, RANK, PANEL):
        columns = [jnp.broadcast_to(arrays[0][:, j + p : j + p + 1], (RANK, 128)) for p in range(PANEL)]
        factors = []
        for p in range(PANEL):
            pivot = columns[p][j + p : j + p + 1]
            diagonal = jnp.where(row_of == j + p, pivot, diagonal)
            factors.append(jnp.where(row_of > j + p, columns[p], 0.0) * (1.0 / pivot))
            for q in range(p + 1, PANEL):
                columns[q] = columns[q] - factors[p] * columns[q][j + p : j + p + 1]
        updated = []
        for array in arrays:
            rows = []
            for p in range(PANEL):
                row = array[j + p : j + p + 1]
                for q in range(p):
                    row = row - factors[q][j + p : j + p + 1] * rows[q]
                rows.append(row)
            for p in range(PANEL):
                array = array - factors[p] * rows[p]
            updated.append(array)
        arrays = updated
    scale = lax.rsqrt(diagonal)
    return [array * scale for array in arrays[1:]]


def swapped(index):
    return index % 2 * 2 + index // 2


def chip_of(near, far, core, shift):
    near, far = swapped(near), swapped(far)
    return (far * NEAR + (near + far * (1 + 2 * core)) % NEAR + shift * core) % (FAR * NEAR)


def split(value):
    high = value.astype(BF16)
    return high, (value - high.astype(F32)).astype(BF16)


def contract_kernel(
    core_ref, factor_ref, tensor_ref, keep_ref, send_ref, left_ref, right_ref, two_ref, held_ref, arrived
):
    first = pltpu.make_async_copy(factor_ref, two_ref, arrived.at[len(PIECES)])
    first.start()
    starts = [sum(PIECES[:p]) for p in range(len(PIECES))]
    copies = [
        pltpu.make_async_copy(tensor_ref.at[pl.ds(start, size)], held_ref.at[pl.ds(start, size)], arrived.at[p])
        for p, (start, size) in enumerate(zip(starts, PIECES))
    ]
    for copy in copies:
        copy.start()
    place = lax.broadcasted_iota(jnp.int32, (RANK, RANK), 0)
    source = lax.broadcasted_iota(jnp.int32, (RANK, RANK), 1)
    near, far = (place // FAR) % NEAR, place % FAR
    core = (core_ref[0] + place // 16) % 2
    wanted = chip_of(near, far, core, SHIFT) * 2 + core
    first.wait()
    high, low = split(nn((source == wanted).astype(F32), two_ref[...]))
    weights = jnp.concatenate([jnp.concatenate([part, part], axis=1) for part in (high, low)], axis=0)
    for copy, start, size in zip(copies, starts, PIECES):
        copy.wait()
        for k in range(start, start + size):
            pieces = jnp.concatenate(split(held_ref[k]), axis=1)
            both = lax.dot_general(weights, pieces, (((1,), (1,)), ((), ())), preferred_element_type=F32)
            value = both[:RANK] + both[RANK:]
            left_ref[pl.ds(k, RANK, stride=RANK), :] = value[:, :128]
            right_ref[pl.ds(k, RANK, stride=RANK), :] = value[:, 128:]
    for q, part_ref in enumerate((left_ref, right_ref)):
        keep_ref[:, 128 * q : 128 * q + 128] = part_ref[: 16 * RANK, :]
        send_ref[:, 128 * q : 128 * q + 128] = part_ref[16 * RANK :, :]


def contract(core, factor_two_t, tensor):
    return pl.pallas_call(
        contract_kernel,
        in_specs=[
            pl.BlockSpec(memory_space=pltpu.SMEM),
            pl.BlockSpec(memory_space=pltpu.HBM),
            pl.BlockSpec(memory_space=pltpu.HBM),
        ],
        out_specs=[pl.BlockSpec(memory_space=pltpu.VMEM)] * 2,
        out_shape=[pltpu.VMEM((16 * RANK, ROWS), F32)] * 2,
        scratch_shapes=[
            pltpu.VMEM((RANK * RANK, 128), F32),
            pltpu.VMEM((RANK * RANK, 128), F32),
            pltpu.VMEM((RANK, COLS), F32),
            pltpu.VMEM((RANK, ROWS, COLS), F32),
            pltpu.SemaphoreType.DMA((len(PIECES) + 1,)),
        ],
        name="contract",
    )(core, factor_two_t, tensor)


def call(kernel, outs, *args, place=pltpu.VMEM):
    return pl.pallas_call(
        kernel,
        in_specs=[pl.BlockSpec(memory_space=pltpu.VMEM)] * len(args),
        out_specs=[pl.BlockSpec(memory_space=pltpu.VMEM)] * len(outs),
        out_shape=[place(shape, F32) for shape in outs],
        name=kernel.__name__,
    )(*[pltpu.with_memory_space_constraint(arg, pltpu.VMEM) for arg in args])


def total_kernel(parts_ref, out_ref):
    out_ref[...] = jnp.sum(parts_ref[...], axis=0)


def start_kernel(parts_ref, old_ref, own_ref, out_ref):
    own = jnp.sum(parts_ref[...], axis=0)
    own_ref[...] = own
    packed = pack(nt(old_ref[...], own))
    for q in range(16):
        out_ref[q] = packed


def weigh_kernel(parts_ref, three_ref, own_ref, out_ref):
    summed = unpack(jnp.sum(parts_ref[...], axis=0))
    three = three_ref[...]
    payload = jnp.concatenate([own_ref[:, :128], own_ref[:, 128:], pack(nt(nn(summed, three), three))], axis=0)
    for q in range(FAR):
        out_ref[q] = payload


def block(held):
    sides = [held[h, q] for h in range(2) for q in range(FAR)]
    rows = [jnp.concatenate([side[:RANK], side[RANK : 2 * RANK]], axis=1) for side in sides]
    return jnp.concatenate(rows, axis=0)


def image_kernel(held_ref, out_ref):
    weights = [unpack(held_ref[h, q, 2 * RANK :]) for h in range(2) for q in range(FAR)]
    image = nn(jnp.concatenate(weights, axis=1), block(held_ref))
    for q in range(NEAR):
        out_ref[q] = image


def project_kernel(parts_ref, held_ref, out_ref):
    image = jnp.sum(parts_ref[...], axis=0)
    projected = nt(image, block(held_ref))
    out = jnp.concatenate([projected[:, :128], projected[:, 128:], pack(nt(image, image))], axis=0)
    for q in range(16):
        out_ref[q] = out


def step_kernel(parts_ref, three_ref, held_ref, out_ref):
    summed = jnp.sum(parts_ref[...], axis=0)
    three = three_ref[...]
    mixing = nt(three, three)
    tiled = jnp.concatenate([jnp.concatenate([mixing] * FAR, axis=0)] * FAR, axis=1)
    left = lax.broadcasted_iota(jnp.int32, tiled.shape, 0) // RANK
    right = lax.broadcasted_iota(jnp.int32, tiled.shape, 1) // RANK
    mixing = jnp.where(left == right, tiled, 0.0)
    weights = [nt(summed[:RANK], mixing), nt(summed[RANK : 2 * RANK], mixing)]
    sides = lower_solve(unpack(summed[2 * RANK :]), weights)
    image = nn(jnp.concatenate(sides, axis=1), block(held_ref))
    for q in range(NEAR):
        out_ref[q] = image


def last_kernel(parts_ref, own_ref, image_ref, out_ref):
    image = jnp.sum(parts_ref[...], axis=0)
    image_ref[...] = image
    out = jnp.concatenate([pack(nt(image, own_ref[...])), pack(nt(image, image))], axis=0)
    for q in range(16):
        out_ref[q] = out


def finish_kernel(parts_ref, image_ref, three_ref, factor_ref, core_ref):
    summed = jnp.sum(parts_ref[...], axis=0)
    coeffs = nn(unpack(summed[:8]), three_ref[...])
    coeffs = jnp.concatenate([coeffs, jnp.zeros((RANK, 128 - RANK), F32)], axis=1)
    left, right, coeffs = lower_solve(unpack(summed[8:]), [image_ref[:, :128], image_ref[:, 128:], coeffs])
    factor_ref[:, :128] = left * math.sqrt(I1)
    factor_ref[:, 128:] = right * math.sqrt(I1)
    core_ref[...] = coeffs[:, :RANK]


def groups(by_far, shift=0):
    found = [[] for _ in range(2 * FAR * NEAR // (FAR if by_far else NEAR))]
    for core in range(2):
        for far in range(FAR):
            for near in range(NEAR):
                chip = chip_of(near, far, core, shift)
                found[(near if by_far else far) * 2 + core].append(chip * 2 + core)
    return found


NEAR_GROUPS = groups(by_far=False)
FAR_GROUPS = groups(by_far=True)
NEAR_SCATTER = groups(by_far=False, shift=SHIFT)
FAR_SCATTER = groups(by_far=True, shift=SHIFT)
ROW_GROUPS = [[10, 5, 0, 15, 6, 9, 12, 3, 2, 13, 8, 7, 14, 1, 4, 11]]
CORES = [[c, c + 1] for c in range(0, 32, 2)]
PAIRS = [(c, c ^ 1) for c in range(32)]


def exchange(values, axis, index_groups=None):
    return lax.all_to_all(values, axis, 0, 0, axis_index_groups=index_groups)


def shards(tensor, old_factor, factor_two, factor_three):
    core = (lax.axis_index("col") & 1).astype(jnp.int32).reshape(1)
    keep, send = contract(core, factor_two.T, tensor)
    value = keep + lax.ppermute(send, "col", PAIRS)
    parts = exchange(value.reshape(NEAR, FAR * RANK, ROWS), "col", NEAR_SCATTER)
    (value,) = call(total_kernel, [(FAR * RANK, ROWS)], parts)
    parts = exchange(value.reshape(FAR, RANK, ROWS), "col", FAR_SCATTER)
    own, parts = call(start_kernel, [(RANK, ROWS), (16, 8, 128)], parts, old_factor.T)
    parts = exchange(parts, "row", ROW_GROUPS)
    (parts,) = call(weigh_kernel, [(FAR, 2 * RANK + 8, 128)], parts, factor_three, own)
    mine = exchange(parts, "col", FAR_GROUPS)
    held = lax.all_gather(mine, "col", axis_index_groups=CORES)
    (parts,) = call(image_kernel, [(NEAR, RANK, ROWS)], held)
    parts = exchange(parts, "col", NEAR_GROUPS)
    (parts,) = call(project_kernel, [(16, 2 * RANK + 8, 128)], parts, held)
    parts = exchange(parts, "row", ROW_GROUPS)
    (parts,) = call(step_kernel, [(NEAR, RANK, ROWS)], parts, factor_three, held)
    parts = exchange(parts, "col", NEAR_GROUPS)
    image, parts = call(last_kernel, [(RANK, ROWS), (16, 16, 128)], parts, own)
    parts = exchange(parts, "row", ROW_GROUPS)
    outs = [(RANK, ROWS), (RANK, RANK)]
    factor, core_part = call(finish_kernel, outs, parts, image, factor_three, place=jax.ShapeDtypeStruct)
    return factor.T, core_part


def solution(mesh):
    return jax.shard_map(
        shards,
        mesh=mesh,
        in_specs=(P(None, "row", "col"), P("row", None), P("col", None), P()),
        out_specs=(P("row", None), P(None, "col")),
        check_vma=False,
    )
```

```python
import math

import jax
import jax.numpy as jnp
from jax import lax
from jax.experimental import pallas as pl
from jax.experimental.pallas import tpu as pltpu
from jax.sharding import PartitionSpec as P

I1 = 4096
RANK = 32
NEAR = 4
FAR = 4
PIECES = (8, 12, 12)
ROWS = 256
COLS = 128
PANEL = 8
SHIFT = 2
HIGHEST = lax.Precision.HIGHEST
F32 = jnp.float32
BF16 = jnp.bfloat16


def nn(a, b):
    return lax.dot_general(a, b, (((1,), (0,)), ((), ())), precision=HIGHEST, preferred_element_type=F32)


def nt(a, b):
    return lax.dot_general(a, b, (((1,), (1,)), ((), ())), precision=HIGHEST, preferred_element_type=F32)


def pack(square):
    return jnp.concatenate([square[8 * q : 8 * q + 8] for q in range(4)], axis=1)


def unpack(packed):
    return jnp.concatenate([packed[:, 32 * q : 32 * q + 32] for q in range(4)], axis=0)


def lower_solve(gram, sides):
    arrays = [jnp.concatenate([gram, jnp.zeros((RANK, 128 - RANK), F32)], axis=1), *sides]
    row_of = lax.broadcasted_iota(jnp.int32, (RANK, 128), 0)
    diagonal = jnp.zeros((RANK, 128), F32)
    for j in range(0, RANK, PANEL):
        columns = [jnp.broadcast_to(arrays[0][:, j + p : j + p + 1], (RANK, 128)) for p in range(PANEL)]
        factors = []
        for p in range(PANEL):
            pivot = columns[p][j + p : j + p + 1]
            diagonal = jnp.where(row_of == j + p, pivot, diagonal)
            factors.append(jnp.where(row_of > j + p, columns[p], 0.0) * (1.0 / pivot))
            for q in range(p + 1, PANEL):
                columns[q] = columns[q] - factors[p] * columns[q][j + p : j + p + 1]
        updated = []
        for array in arrays:
            rows = []
            for p in range(PANEL):
                row = array[j + p : j + p + 1]
                for q in range(p):
                    row = row - factors[q][j + p : j + p + 1] * rows[q]
                rows.append(row)
            for p in range(PANEL):
                array = array - factors[p] * rows[p]
            updated.append(array)
        arrays = updated
    scale = lax.rsqrt(diagonal)
    return [array * scale for array in arrays[1:]]


def swapped(index):
    return index % 2 * 2 + index // 2


def chip_of(near, far, core, shift):
    near, far = swapped(near), swapped(far)
    return (far * NEAR + (near + far * (1 + 2 * core)) % NEAR + shift * core) % (FAR * NEAR)


def split(value):
    high = value.astype(BF16)
    return high, (value - high.astype(F32)).astype(BF16)


def contract_kernel(
    core_ref, factor_ref, tensor_ref, keep_ref, send_ref, left_ref, right_ref, two_ref, held_ref, arrived
):
    first = pltpu.make_async_copy(factor_ref, two_ref, arrived.at[len(PIECES)])
    first.start()
    starts = [sum(PIECES[:p]) for p in range(len(PIECES))]
    copies = [
        pltpu.make_async_copy(tensor_ref.at[pl.ds(start, size)], held_ref.at[pl.ds(start, size)], arrived.at[p])
        for p, (start, size) in enumerate(zip(starts, PIECES))
    ]
    for copy in copies:
        copy.start()
    place = lax.broadcasted_iota(jnp.int32, (RANK, RANK), 0)
    source = lax.broadcasted_iota(jnp.int32, (RANK, RANK), 1)
    near, far = (place // FAR) % NEAR, place % FAR
    core = (core_ref[0] + place // 16) % 2
    wanted = chip_of(near, far, core, SHIFT) * 2 + core
    first.wait()
    high, low = split(nn((source == wanted).astype(F32), two_ref[...]))
    weights = jnp.concatenate([jnp.concatenate([part, part], axis=1) for part in (high, low)], axis=0)
    for copy, start, size in zip(copies, starts, PIECES):
        copy.wait()
        for k in range(start, start + size):
            pieces = jnp.concatenate(split(held_ref[k]), axis=1)
            both = lax.dot_general(weights, pieces, (((1,), (1,)), ((), ())), preferred_element_type=F32)
            value = both[:RANK] + both[RANK:]
            left_ref[pl.ds(k, RANK, stride=RANK), :] = value[:, :128]
            right_ref[pl.ds(k, RANK, stride=RANK), :] = value[:, 128:]
    for q, part_ref in enumerate((left_ref, right_ref)):
        keep_ref[:, 128 * q : 128 * q + 128] = part_ref[: 16 * RANK, :]
        send_ref[:, 128 * q : 128 * q + 128] = part_ref[16 * RANK :, :]


def contract(core, factor_two_t, tensor):
    return pl.pallas_call(
        contract_kernel,
        in_specs=[
            pl.BlockSpec(memory_space=pltpu.SMEM),
            pl.BlockSpec(memory_space=pltpu.HBM),
            pl.BlockSpec(memory_space=pltpu.HBM),
        ],
        out_specs=[pl.BlockSpec(memory_space=pltpu.VMEM)] * 2,
        out_shape=[pltpu.VMEM((16 * RANK, ROWS), F32)] * 2,
        scratch_shapes=[
            pltpu.VMEM((RANK * RANK, 128), F32),
            pltpu.VMEM((RANK * RANK, 128), F32),
            pltpu.VMEM((RANK, COLS), F32),
            pltpu.VMEM((RANK, ROWS, COLS), F32),
            pltpu.SemaphoreType.DMA((len(PIECES) + 1,)),
        ],
        name="contract",
    )(core, factor_two_t, tensor)


def call(kernel, outs, *args, place=pltpu.VMEM):
    return pl.pallas_call(
        kernel,
        in_specs=[pl.BlockSpec(memory_space=pltpu.VMEM)] * len(args),
        out_specs=[pl.BlockSpec(memory_space=pltpu.VMEM)] * len(outs),
        out_shape=[place(shape, F32) for shape in outs],
        name=kernel.__name__,
    )(*[pltpu.with_memory_space_constraint(arg, pltpu.VMEM) for arg in args])


def total_kernel(parts_ref, out_ref):
    out_ref[...] = jnp.sum(parts_ref[...], axis=0)


def start_kernel(parts_ref, old_ref, own_ref, out_ref):
    own = jnp.sum(parts_ref[...], axis=0)
    own_ref[...] = own
    packed = pack(nt(old_ref[...], own))
    for q in range(16):
        out_ref[q] = packed


def weigh_kernel(parts_ref, three_ref, own_ref, out_ref):
    summed = unpack(jnp.sum(parts_ref[...], axis=0))
    three = three_ref[...]
    payload = jnp.concatenate([own_ref[:, :128], own_ref[:, 128:], pack(nt(nn(summed, three), three))], axis=0)
    for q in range(FAR):
        out_ref[q] = payload


def block(held):
    sides = [held[h, q] for h in range(2) for q in range(FAR)]
    rows = [jnp.concatenate([side[:RANK], side[RANK : 2 * RANK]], axis=1) for side in sides]
    return jnp.concatenate(rows, axis=0)


def image_kernel(held_ref, out_ref):
    weights = [unpack(held_ref[h, q, 2 * RANK :]) for h in range(2) for q in range(FAR)]
    image = nn(jnp.concatenate(weights, axis=1), block(held_ref))
    for q in range(NEAR):
        out_ref[q] = image


def project_kernel(parts_ref, held_ref, out_ref):
    image = jnp.sum(parts_ref[...], axis=0)
    projected = nt(image, block(held_ref))
    out = jnp.concatenate([projected[:, :128], projected[:, 128:], pack(nt(image, image))], axis=0)
    for q in range(16):
        out_ref[q] = out


def step_kernel(parts_ref, three_ref, held_ref, out_ref):
    summed = jnp.sum(parts_ref[...], axis=0)
    three = three_ref[...]
    mixing = nt(three, three)
    tiled = jnp.concatenate([jnp.concatenate([mixing] * FAR, axis=0)] * FAR, axis=1)
    left = lax.broadcasted_iota(jnp.int32, tiled.shape, 0) // RANK
    right = lax.broadcasted_iota(jnp.int32, tiled.shape, 1) // RANK
    mixing = jnp.where(left == right, tiled, 0.0)
    weights = [nt(summed[:RANK], mixing), nt(summed[RANK : 2 * RANK], mixing)]
    sides = lower_solve(unpack(summed[2 * RANK :]), weights)
    image = nn(jnp.concatenate(sides, axis=1), block(held_ref))
    for q in range(NEAR):
        out_ref[q] = image


def last_kernel(parts_ref, own_ref, image_ref, out_ref):
    image = jnp.sum(parts_ref[...], axis=0)
    image_ref[...] = image
    out = jnp.concatenate([pack(nt(image, own_ref[...])), pack(nt(image, image))], axis=0)
    for q in range(16):
        out_ref[q] = out


def finish_kernel(parts_ref, image_ref, three_ref, factor_ref, core_ref):
    summed = jnp.sum(parts_ref[...], axis=0)
    coeffs = nn(unpack(summed[:8]), three_ref[...])
    coeffs = jnp.concatenate([coeffs, jnp.zeros((RANK, 128 - RANK), F32)], axis=1)
    left, right, coeffs = lower_solve(unpack(summed[8:]), [image_ref[:, :128], image_ref[:, 128:], coeffs])
    factor_ref[:, :128] = left * math.sqrt(I1)
    factor_ref[:, 128:] = right * math.sqrt(I1)
    core_ref[...] = coeffs[:, :RANK]


def groups(by_far, shift=0):
    found = [[] for _ in range(2 * FAR * NEAR // (FAR if by_far else NEAR))]
    for core in range(2):
        for far in range(FAR):
            for near in range(NEAR):
                chip = chip_of(near, far, core, shift)
                found[(near if by_far else far) * 2 + core].append(chip * 2 + core)
    return found


NEAR_GROUPS = groups(by_far=False)
FAR_GROUPS = groups(by_far=True)
NEAR_GATHER = [group[:: 1 - 2 * (group[0] % 2)] for group in NEAR_GROUPS]
FAR_GATHER = [group[:: 1 - 2 * (group[0] % 2)] for group in FAR_GROUPS]
NEAR_SCATTER = groups(by_far=False, shift=SHIFT)
FAR_SCATTER = groups(by_far=True, shift=SHIFT)
ROW_GROUPS = [[10, 5, 0, 15, 6, 9, 12, 3, 2, 13, 8, 7, 14, 1, 4, 11]]
CORES = [[c, c + 1] for c in range(0, 32, 2)]
PAIRS = [(c, c ^ 1) for c in range(32)]


def exchange(values, axis, index_groups=None):
    return lax.all_to_all(values, axis, 0, 0, axis_index_groups=index_groups)


def shards(tensor, old_factor, factor_two, factor_three):
    core = (lax.axis_index("col") & 1).astype(jnp.int32).reshape(1)
    keep, send = contract(core, factor_two.T, tensor)
    value = keep + lax.ppermute(send, "col", PAIRS)
    parts = exchange(value.reshape(NEAR, FAR * RANK, ROWS), "col", NEAR_SCATTER)
    (value,) = call(total_kernel, [(FAR * RANK, ROWS)], parts)
    parts = exchange(value.reshape(FAR, RANK, ROWS), "col", FAR_SCATTER)
    own, parts = call(start_kernel, [(RANK, ROWS), (16, 8, 128)], parts, old_factor.T)
    parts = exchange(parts, "row", ROW_GROUPS)
    (parts,) = call(weigh_kernel, [(FAR, 2 * RANK + 8, 128)], parts, factor_three, own)
    mine = exchange(parts, "col", FAR_GATHER)
    held = lax.all_gather(mine, "col", axis_index_groups=CORES)
    (parts,) = call(image_kernel, [(NEAR, RANK, ROWS)], held)
    parts = exchange(parts, "col", NEAR_GATHER)
    (parts,) = call(project_kernel, [(16, 2 * RANK + 8, 128)], parts, held)
    parts = exchange(parts, "row", ROW_GROUPS)
    (parts,) = call(step_kernel, [(NEAR, RANK, ROWS)], parts, factor_three, held)
    parts = exchange(parts, "col", NEAR_GATHER)
    image, parts = call(last_kernel, [(RANK, ROWS), (16, 16, 128)], parts, own)
    parts = exchange(parts, "row", ROW_GROUPS)
    outs = [(RANK, ROWS), (RANK, RANK)]
    factor, core_part = call(finish_kernel, outs, parts, image, factor_three, place=jax.ShapeDtypeStruct)
    return factor.T, core_part


def solution(mesh):
    return jax.shard_map(
        shards,
        mesh=mesh,
        in_specs=(P(None, "row", "col"), P("row", None), P("col", None), P()),
        out_specs=(P("row", None), P(None, "col")),
        check_vma=False,
    )
```
